32 devices in a mesh: group: 2 (over y), ctx: 8 (over z, x), head: 2 (over core).
Axes of the slice: x: 2, y: 2, z: 4, core: 2. Of those that a mesh axis runs over, the one named last changes fastest.
Arguments:
- queries: bfloat16 [4096, 4096], P(('group', 'ctx'), 'head'), parts along dimension 0, may hold values from -7 to 7
- keys: bfloat16 [4096, 1024], P(('group', 'ctx'), 'head'), parts along dimension 0, may hold values from -4 to 4
- values: bfloat16 [4096, 1024], P(('group', 'ctx'), 'head'), parts along dimension 0, may hold values from -24 to 24
- doc_of_block: int32 [32], P('group'), parts along dimension 0, may hold values from 0 to 4, never falling along the last dimension, each value on 1 to 8 neighbouring positions
- out_weight: bfloat16 [4096, 4096], P('ctx', 'head'), may hold values from -0.09375 to 0.09375
Outputs:
- mixed: bfloat16 [4096, 4096], P(('group', 'ctx'), 'head'), parts along dimension 0
The draws below stay inside these ranges and needn't reach their ends.
There are 2 independent parts, one for each index of `group`. The reference program is written for one: setup_inputs(seed, part) draws one part's arguments, and reference() takes and returns one part's arrays. A program takes and returns all parts, laid end to end along the dimension named above; an argument that names none is the same for every part. Nothing has to cross between parts.
Inputs may be any that keep to these rules, and one draw needn't show every extreme that they name: `doc_of_block`: blocks of one document are consecutive, and a document covers at most 8 blocks.
All inputs are finite; a program needn't handle non-finite values.
Results may differ from the reference program's by a relative error of at most 0.006.
Values may be sent and summed in bfloat16 or wider, within the bound.
A program may use at most 64 MiB of HBM per device.

```python
import math
import jax
import jax.numpy as jnp
import numpy as np
from jax import lax

D = 4096
QUERY_HEADS = 32
KEY_VALUE_HEADS = 8
HEAD_SIZE = 128
BLOCK_TOKENS = 128
PACKED_TOKENS = 2048
NBLK = 16
DOCB = 8
DOCS = 5


def draw_keys(key, part):
    local_shape = (PACKED_TOKENS, KEY_VALUE_HEADS * HEAD_SIZE)
    drawn = jnp.clip(jax.random.normal(jax.random.fold_in(key, 1), local_shape, jnp.float32), -4.0, 4.0)
    return drawn.astype(jnp.bfloat16)


def draw_queries(key, part):
    local_shape = (PACKED_TOKENS, QUERY_HEADS * HEAD_SIZE)
    drawn = jnp.clip(1.5 * jax.random.normal(jax.random.fold_in(key, 2), local_shape, jnp.float32), -7.0, 7.0)
    return drawn.astype(jnp.bfloat16)


def block_scale(own_key, extent, shards, least, top_value):
    loudness = 1.0
    for dim, shards_of in shards:
        steps = jax.random.uniform(jax.random.fold_in(jax.random.fold_in(own_key, 6), dim), (shards_of,), jnp.float32, least / len(shards), top_value / len(shards))
        loudness = loudness * jnp.repeat(jnp.exp(steps), extent[dim] // shards_of).reshape((-1,) + (1,) * (len(extent) - 1 - dim))
    return loudness


def split_up(count, total, most, lean):
    loads = [(1 << 20) // math.isqrt(grade ** lean) + 1 for grade in range(2, count + 1)]
    surplus, given = total - most - (count - 1), [1] * (count - 1)
    while surplus > 0:
        movable = [i for i in range(count - 1) if given[i] < most]
        pool, left = sum([loads[i] for i in movable]), surplus
        for i in movable:
            extra = min(most - given[i], max(1, left * loads[i] // pool), surplus)
            given[i] = given[i] + extra
            surplus = surplus - extra
    return np.array([most] + given)


def ragged_sizes(rng, count, total, most, skew):
    if count == 2:
        one = jax.random.randint(rng, (), max(1, total - most), min(most, total - 1) + 1)
        return jnp.stack([one, total - one])
    tallies = jnp.asarray(split_up(count, total, most, skew), jnp.int32)
    pairs = (count - 1) // 2
    source_of, sink = tallies[1:1 + 2 * pairs:2], tallies[2:2 + 2 * pairs:2]
    margin = jnp.minimum(source_of - 1, most - sink)
    passed = jax.random.randint(jax.random.fold_in(rng, 1), (pairs,), 0, 1 << 20) % (margin + 1)
    tallies = tallies.at[1:1 + 2 * pairs:2].set(source_of - passed).at[2:2 + 2 * pairs:2].set(sink + passed)
    return tallies[jax.random.permutation(jax.random.fold_in(rng, 2), count)]


def scatter_about(own_key, shape, width, reach, pieces=(), held_as=jnp.bfloat16):
    array = width * jax.random.normal(own_key, shape, jnp.float32)
    if pieces:
        array = array * block_scale(own_key, shape, pieces, -0.22, 0.18)
    return jnp.clip(array, -reach, reach).astype(held_as)


def setup_inputs(seed: int = 0, part: int = 0) -> dict:
    splits = jax.random.split(jax.random.key(seed), 6)
    own_keys = jax.random.split(jax.random.fold_in(splits[5], part), 6)
    queries = draw_queries(jax.random.fold_in(jax.random.fold_in(splits[5], part), 71), part)
    keys = draw_keys(jax.random.fold_in(jax.random.fold_in(splits[5], part), 71), part)
    values = scatter_about(own_keys[2], (PACKED_TOKENS, KEY_VALUE_HEADS * HEAD_SIZE), 4.0, 24.0, ((0, 8), (1, 2)))
    doc_of_block = jnp.searchsorted(jnp.cumsum(ragged_sizes(own_keys[3], DOCS, NBLK, DOCB, 2)), jnp.arange(NBLK), side="right").astype(jnp.int32)
    out_weight = scatter_about(splits[4], (QUERY_HEADS * HEAD_SIZE, D), (QUERY_HEADS * HEAD_SIZE) ** -0.5, 0.09375, ((0, 8), (1, 2)))
    return dict(queries=queries, keys=keys, values=values, doc_of_block=doc_of_block, out_weight=out_weight)


def reference(queries, keys, values, doc_of_block, out_weight):
    group_width = QUERY_HEADS // KEY_VALUE_HEADS
    score_scale = 1.0 / math.sqrt(HEAD_SIZE)
    same_doc = doc_of_block[:, None] == doc_of_block[None, :]
    first_block = jnp.argmax(same_doc, axis=1).astype(jnp.int32)
    offsets = jnp.arange(BLOCK_TOKENS, dtype=jnp.int32)

    def one_block(block_index):
        query_row_block = lax.dynamic_slice_in_dim(queries, block_index * BLOCK_TOKENS, BLOCK_TOKENS, 0)
        query_head_rows = query_row_block.astype(jnp.float32).reshape(BLOCK_TOKENS, KEY_VALUE_HEADS, group_width, HEAD_SIZE)
        query_pos = block_index * BLOCK_TOKENS + offsets

        def block_scores(key_block):
            key_row_block = lax.dynamic_slice_in_dim(keys, key_block * BLOCK_TOKENS, BLOCK_TOKENS, 0)
            key_head_rows = key_row_block.astype(jnp.float32).reshape(BLOCK_TOKENS, KEY_VALUE_HEADS, HEAD_SIZE)
            scores = jnp.einsum('qhgd,khd->hgqk', query_head_rows, key_head_rows) * score_scale
            key_pos = key_block * BLOCK_TOKENS + offsets
            causal = key_pos[None, :] <= query_pos[:, None]
            return jnp.where(causal, scores, -jnp.inf)

        def take_max(key_block, running_max):
            return jnp.maximum(running_max, lax.optimization_barrier(jnp.max(block_scores(key_block), axis=-1)))
        initial_maximum = jnp.full((KEY_VALUE_HEADS, group_width, BLOCK_TOKENS), -jnp.inf, dtype=jnp.float32)
        row_max = lax.fori_loop(first_block[block_index], block_index + 1, take_max, initial_maximum)

        def accumulate(key_block, state_now):
            summed, totals = state_now
            weights = jnp.exp(block_scores(key_block) - row_max[..., None])
            rounded = lax.optimization_barrier(weights.astype(jnp.bfloat16)).astype(jnp.float32)
            value_row_block = lax.dynamic_slice_in_dim(values, key_block * BLOCK_TOKENS, BLOCK_TOKENS, 0)
            value_head_rows = value_row_block.astype(jnp.float32).reshape(BLOCK_TOKENS, KEY_VALUE_HEADS, HEAD_SIZE)
            summed = summed + jnp.einsum('hgqk,khd->hgqd', rounded, value_head_rows)
            totals = totals + lax.optimization_barrier(jnp.sum(weights, axis=-1))
            return (summed, totals)
        initial_state = (jnp.zeros((KEY_VALUE_HEADS, group_width, BLOCK_TOKENS, HEAD_SIZE), jnp.float32), jnp.zeros((KEY_VALUE_HEADS, group_width, BLOCK_TOKENS), jnp.float32))
        summed, totals = lax.fori_loop(first_block[block_index], block_index + 1, accumulate, initial_state)
        attended = summed / totals[..., None]
        return jnp.transpose(attended, (2, 0, 1, 3)).reshape(BLOCK_TOKENS, QUERY_HEADS * HEAD_SIZE).astype(jnp.bfloat16)
    attended = lax.map(one_block, jnp.arange(NBLK, dtype=jnp.int32)).reshape(PACKED_TOKENS, QUERY_HEADS * HEAD_SIZE)
    return jnp.dot(attended, out_weight, preferred_element_type=jnp.float32).astype(jnp.bfloat16)
```

```python
import math

import jax
import jax.numpy as jnp
from jax import lax
from jax.sharding import PartitionSpec as P

HEAD_SIZE = 128
BLOCK_TOKENS = 128


def passed_along(array, axis, by):
    peers = lax.axis_size(axis)
    pairs = [(i, i + by) for i in range(peers) if 0 <= i + by < peers]
    return lax.ppermute(array, axis, pairs)


def lookup_docs(positions, doc_of_block):
    block_ids = jnp.floor_divide(positions, BLOCK_TOKENS)
    table_ids = jnp.arange(doc_of_block.shape[0], dtype=jnp.int32)
    matches = block_ids[:, None] == table_ids[None, :]
    return jnp.max(jnp.where(matches, doc_of_block[None, :], -1), axis=1)


def update(state_now, query_head_rows, key_piece, value_piece, visible):
    running_max, summed, totals = state_now
    rows_here = key_piece.shape[0]
    kv_heads = query_head_rows.shape[1]
    key_head_rows = key_piece.reshape(rows_here, kv_heads, HEAD_SIZE)
    value_head_rows = value_piece.reshape(rows_here, kv_heads, HEAD_SIZE)
    score_scale = 1.0 / math.sqrt(HEAD_SIZE)
    scores = (
        jnp.einsum(
            "qhgd,khd->hgqk", query_head_rows, key_head_rows, preferred_element_type=jnp.float32
        )
        * score_scale
    )
    scores = jnp.where(visible, scores, -1e30)
    new_max = jnp.maximum(running_max, jnp.max(scores, axis=-1))
    weights = jnp.where(visible, jnp.exp(scores - new_max[..., None]), 0.0)
    rescale = jnp.exp(running_max - new_max)
    products = jnp.einsum(
        "hgqk,khd->hgqd",
        weights.astype(jnp.bfloat16),
        value_head_rows,
        preferred_element_type=jnp.float32,
    )
    summed = summed * rescale[..., None] + products
    totals = totals * rescale + jnp.sum(weights, axis=-1)
    return (new_max, summed, totals)


def fresh_state(kv_heads, group_width, rows_here):
    return (
        jnp.full((kv_heads, group_width, rows_here), -1e30, jnp.float32),
        jnp.zeros((kv_heads, group_width, rows_here, HEAD_SIZE), jnp.float32),
        jnp.zeros((kv_heads, group_width, rows_here), jnp.float32),
    )


def finish(state_now, rows_here, q_heads):
    running_max, summed, totals = state_now
    attended = summed / totals[..., None]
    return (
        jnp.transpose(attended, (2, 0, 1, 3))
        .reshape(rows_here, q_heads * HEAD_SIZE)
        .astype(jnp.bfloat16)
    )


def per_device(queries, keys, values, doc_of_block, out_weight):
    tok_rows = queries.shape[0]
    kv_heads = keys.shape[1] // HEAD_SIZE
    q_heads = queries.shape[1] // HEAD_SIZE
    group_width = q_heads // kv_heads
    ctx_count = lax.axis_size("ctx")
    reach_devs = min(8, ctx_count // 2)
    ctx_index = lax.axis_index("ctx")
    part_cols = out_weight.shape[1] // lax.axis_size("group")
    weight_part = lax.dynamic_slice_in_dim(
        out_weight, lax.axis_index("group") * part_cols, part_cols, 1
    )
    weight_part = lax.all_gather(weight_part, "ctx", axis=0, tiled=True)
    query_start = ctx_index * tok_rows
    query_pos = query_start + jnp.arange(tok_rows, dtype=jnp.int32)
    query_doc = lookup_docs(query_pos, doc_of_block)
    query_head_rows = queries.reshape(tok_rows, kv_heads, group_width, HEAD_SIZE)

    def attend(state_now, key_piece, value_piece, key_start):
        key_pos = key_start + jnp.arange(key_piece.shape[0], dtype=jnp.int32)
        key_doc = lookup_docs(key_pos, doc_of_block)
        visible = (key_doc[None, :] == query_doc[:, None]) & (
            key_pos[None, :] <= query_pos[:, None]
        )
        return update(state_now, query_head_rows, key_piece, value_piece, visible)

    initial_state = fresh_state(kv_heads, group_width, tok_rows)
    state_now = attend(initial_state, keys, values, query_start)
    for distance in range(1, reach_devs + 1):
        prior_keys, prior_values = passed_along((keys, values), "ctx", distance)
        state_now = attend(state_now, prior_keys, prior_values, query_start - distance * tok_rows)
    attended = finish(state_now, tok_rows, q_heads)
    groups, heads = lax.axis_size("group"), lax.axis_size("head")
    group_index, head_index = lax.axis_index("group"), lax.axis_index("head")
    width = attended.shape[1]
    mixed = jnp.zeros((tok_rows, groups * part_cols), jnp.bfloat16)
    for dg in range(groups):
        total = None
        for dh in range(heads):
            piece = attended
            if dg or dh:
                pairs = [
                    (a * heads + b, (a + dg) % groups * heads + (b + dh) % heads)
                    for a in range(groups)
                    for b in range(heads)
                ]
                piece = lax.ppermute(attended, ("group", "head"), pairs)
            source = lax.rem(head_index - dh + heads, heads)
            rows = lax.dynamic_slice_in_dim(weight_part, source * width, width, 0)
            product = jnp.dot(piece, rows, preferred_element_type=jnp.float32)
            total = product if total is None else total + product
        share = total.astype(jnp.bfloat16)
        if dg:
            share = lax.ppermute(share, "group", [(a, (a - dg) % groups) for a in range(groups)])
        column = lax.rem(group_index + dg, groups) * part_cols
        mixed = lax.dynamic_update_slice(mixed, share, (0, column))
    return mixed


def solution(mesh):
    return jax.shard_map(
        per_device,
        mesh=mesh,
        in_specs=(
            P(("group", "ctx"), "head"),
            P(("group", "ctx"), "head"),
            P(("group", "ctx"), "head"),
            P("group"),
            P("ctx", "head"),
        ),
        out_specs=P(("group", "ctx"), "head"),
        check_vma=False,
    )
```

```python
import functools
import math

import jax
import jax.numpy as jnp
from jax import lax
from jax.experimental import pallas as pl
from jax.experimental.pallas import tpu as pltpu
from jax.sharding import PartitionSpec as P

HEAD_SIZE = 128
BLOCK_TOKENS = 128
MESH = pl.DeviceIdType.MESH


def fused(
    groups, ctx_count, heads, reach,
    q_ref, k_ref, v_ref, bias_ref, w_ref, out_ref,
    kv, wbuf, abuf, cbuf, crecv, local_sem,
    line_send, line_recv, mate_send, mate_recv,
    wmate_send, wmate_recv, wline_send, wline_recv,
    plane_send, plane_recv, core_send, core_recv, c_send, c_recv,
):
    g, c, h = lax.axis_index("group"), lax.axis_index("ctx"), lax.axis_index("head")
    x, z = lax.rem(c, 2), c // 2
    lines, steps = ctx_count // 2, reach // 2
    tok = q_ref.shape[0]
    kv_heads = k_ref.shape[1] // HEAD_SIZE
    group_width = q_ref.shape[1] // k_ref.shape[1]
    chunk = group_width * HEAD_SIZE
    shard = w_ref.shape[0]
    part = wbuf.shape[1]
    parts = 2 * groups
    me = g * 2 + x
    mate = c + 1 - 2 * x
    offsets = [(dg, dx) for dg in range(groups) for dx in range(2) if dg or dx]

    def copy(src, dst, send, recv, device):
        return pltpu.make_async_remote_copy(
            src_ref=src, dst_ref=dst, send_sem=send, recv_sem=recv,
            device_id=device, device_id_type=MESH,
        )

    def guarded(condition, action):
        if condition is None:
            action()
        else:
            pl.when(condition)(action)

    barrier = pltpu.get_barrier_semaphore()

    def greet(device):
        pl.semaphore_signal(barrier, inc=1, device_id=device, device_id_type=MESH)

    def plane_to(dg, dx):
        return (lax.rem(g + dg, groups), 2 * z + lax.rem(x + dx, 2), h)

    def plane_from(dg, dx):
        return lax.rem(g - dg + groups, groups) * 2 + lax.rem(x + dx, 2)

    for dg, dx in offsets:
        greet(plane_to(dg, dx))
    for dh in range(1, heads):
        greet((g, c, lax.rem(h + dh, heads)))
    up, down = z + 1 < lines, z >= 1
    pl.when(up)(lambda: greet((g, c + 2, h)))
    pl.when(down)(lambda: greet((g, c - 2, h)))
    pl.semaphore_wait(
        barrier, len(offsets) + heads - 1 + up.astype(jnp.int32) + down.astype(jnp.int32)
    )

    pending = []

    def start(condition, make):
        guarded(condition, lambda: make().start())
        pending.append((condition, make))

    def received(condition, make):
        guarded(condition, lambda: make().wait_recv())

    kv[0, 0] = k_ref[...]
    kv[0, 1] = v_ref[...]

    def line_copy(s):
        return lambda: copy(
            kv.at[2 * (s - 1)], kv.at[2 * s], line_send.at[s - 1], line_recv.at[s - 1], (g, c + 2, h)
        )

    def mate_copy(m, side):
        return lambda: copy(
            kv.at[2 * m + 2 * side], kv.at[2 * m + 1], mate_send.at[m], mate_recv.at[m], (g, mate, h)
        )

    start(up, line_copy(1))
    start(x == 0, mate_copy(0, 0))

    def rows_of(source):
        return pl.ds(pl.multiple_of(source * shard, shard), shard)

    def columns_of(which):
        return pl.ds(pl.multiple_of(which * part, part), part)

    own = pltpu.make_async_copy(w_ref.at[:, columns_of(me)], wbuf.at[rows_of(c)], local_sem)
    own.start()

    def wmate_copy():
        return copy(
            w_ref.at[:, columns_of(g * 2 + 1 - x)], wbuf.at[rows_of(c)],
            wmate_send, wmate_recv, (g, mate, h),
        )

    start(None, wmate_copy)

    def wline_copy(way, s, which):
        def make():
            line = z - s if way == 0 else z + s
            source = 2 * line + (x if which == 0 else 1 - x)
            rows = rows_of(source)
            to = c + 2 if way == 0 else c - 2
            return copy(
                wbuf.at[rows], wbuf.at[rows],
                wline_send.at[way, s, which], wline_recv.at[way, s, which], (g, to, h),
            )
        return make

    def wline_sends(way, s):
        if way == 0:
            return up & (z >= s)
        return down & (z + s < lines)

    def wline_arrives(way, s):
        return z >= s + 1 if way == 0 else z + s + 1 < lines

    def pump_weights(s):
        for which in range(2):
            for way in range(2):
                received(wline_arrives(way, s), wline_copy(way, s, which))
                if s + 1 < lines - 1:
                    start(wline_sends(way, s + 1), wline_copy(way, s + 1, which))

    own.wait()
    for way in (1, 0):
        start(wline_sends(way, 0), wline_copy(way, 0, 0))

    for s in range(1, steps + 1):
        received(z >= s, line_copy(s))
        if s < steps:
            start(up & (z >= s), line_copy(s + 1))
            start((x == 0) & (z >= s), mate_copy(s, 0))
        start((x == 1) & (z >= s), mate_copy(s - 1, 1))
    received(None, wmate_copy)
    for way in (1, 0):
        start(wline_sends(way, 0), wline_copy(way, 0, 1))
    for m in range(steps):
        received(c >= 2 * m + 1, mate_copy(m, 0))
    for d in range(1, reach + 1):

        @pl.when(c < d)
        def _():
            kv[d] = jnp.zeros(kv.shape[1:], kv.dtype)

    scale = math.log2(math.e) / math.sqrt(HEAD_SIZE)

    def slot(d, which, column):
        rows = pl.ds(0, tok) if d < reach else pl.ds(tok - BLOCK_TOKENS, BLOCK_TOKENS)
        return kv[d, which, rows, column]

    def plane_copy(hk, i):
        def make():
            j = h * kv_heads + hk
            return copy(
                abuf.at[me, j], abuf.at[me, j],
                plane_send.at[i, hk], plane_recv.at[i, hk], plane_to(*offsets[i]),
            )
        return make

    def core_copy(hk, i, dh):
        def make():
            p = me if i == len(offsets) else plane_from(*offsets[i])
            j = h * kv_heads + hk
            return copy(
                abuf.at[p, j], abuf.at[p, j],
                core_send.at[i, hk, dh - 1], core_recv.at[i, hk, dh - 1],
                (g, c, lax.rem(h + dh, heads)),
            )
        return make

    def relay(hk):
        for i in range(len(offsets)):
            received(None, plane_copy(hk, i))
            for dh in range(1, heads):
                start(None, core_copy(hk, i, dh))

    pumped = 0
    for hk in range(kv_heads):
        column = pl.ds(hk * HEAD_SIZE, HEAD_SIZE)

        @pl.loop(0, group_width)
        def _(n):
            at = pl.multiple_of(hk * chunk + n * HEAD_SIZE, HEAD_SIZE)
            query = q_ref[:, pl.ds(at, HEAD_SIZE)]
            scores, top = [], None
            for d in range(reach + 1):
                keys = slot(d, 0, column)
                s = lax.dot_general(
                    query, keys, (((1,), (1,)), ((), ())), preferred_element_type=jnp.float32
                )
                s = s + bias_ref[:, pl.ds(d * tok, keys.shape[0])]
                scores.append(s)
                high = jnp.max(s, axis=-1, keepdims=True)
                top = high if top is None else jnp.maximum(top, high)
            total, summed = None, None
            for d in range(reach + 1):
                weights = jnp.exp2((scores[d] - top) * scale)
                t = jnp.sum(weights, axis=-1, keepdims=True)
                o = jnp.dot(
                    weights.astype(jnp.bfloat16), slot(d, 1, column),
                    preferred_element_type=jnp.float32,
                )
                total = t if total is None else total + t
                summed = o if summed is None else summed + o
            to = pl.multiple_of(n * HEAD_SIZE, HEAD_SIZE)
            abuf[me, h * kv_heads + hk, :, pl.ds(to, HEAD_SIZE)] = (summed / total).astype(
                jnp.bfloat16
            )

        for i in reversed(range(len(offsets))):
            start(None, plane_copy(hk, i))
        for dh in range(1, heads):
            start(None, core_copy(hk, len(offsets), dh))
        if hk % 2 == 0 and pumped < lines - 2:
            pump_weights(pumped)
            pumped += 1
        if hk >= 2:
            relay(hk - 2)
    for hk in range(max(kv_heads - 2, 0), kv_heads):
        relay(hk)
    while pumped < lines - 1:
        pump_weights(pumped)
        pumped += 1
    for hk in range(kv_heads):
        for i in range(len(offsets) + 1):
            for dh in range(1, heads):
                received(None, core_copy(hk, i, dh))

    def c_copy(i):
        def make():
            dg, dx = offsets[i]
            return copy(cbuf.at[i], crecv.at[me], c_send.at[i], c_recv.at[i], plane_to(dg, dx))
        return make

    def project(p):
        total = None
        for j in range(heads * kv_heads):
            product = jnp.dot(
                abuf[p, j], wbuf[j * chunk:(j + 1) * chunk, :], preferred_element_type=jnp.float32
            )
            total = product if total is None else total + product
        return total.astype(jnp.bfloat16)

    for i in reversed(range(len(offsets))):
        dg, dx = offsets[i]
        cbuf[i] = project(lax.rem(g + dg, groups) * 2 + lax.rem(x + dx, 2))
        start(None, c_copy(i))
    out_ref[:, columns_of(me)] = project(me)
    for i in reversed(range(len(offsets))):
        received(None, c_copy(i))
        source = plane_from(*offsets[i])
        out_ref[:, columns_of(source)] = crecv[source]
    for condition, make in pending:
        guarded(condition, lambda make=make: make().wait_send())


def per_device(queries, keys, values, doc_of_block, out_weight):
    tok = queries.shape[0]
    kv_heads = keys.shape[1] // HEAD_SIZE
    groups, ctx_count, heads = (lax.axis_size(a) for a in ("group", "ctx", "head"))
    reach = min(8, ctx_count // 2)
    lines, steps = ctx_count // 2, reach // 2
    parts = 2 * groups
    part = out_weight.shape[1] // parts
    chunk = queries.shape[1] // kv_heads
    start = lax.axis_index("ctx") * tok
    query_pos = start + jnp.arange(tok, dtype=jnp.int32)
    key_pos = jnp.concatenate(
        [
            start - d * tok + jnp.arange(0 if d < reach else tok - BLOCK_TOKENS, tok, dtype=jnp.int32)
            for d in range(reach + 1)
        ]
    )
    table = jnp.arange(doc_of_block.shape[0], dtype=jnp.int32)

    def docs(positions):
        matches = jnp.floor_divide(positions, BLOCK_TOKENS)[:, None] == table[None, :]
        return jnp.max(jnp.where(matches, doc_of_block[None, :], -1), axis=1)

    visible = (docs(key_pos)[None, :] == docs(query_pos)[:, None]) & (
        key_pos[None, :] <= query_pos[:, None]
    )
    bias = jnp.where(visible, 0.0, -1e30).astype(jnp.float32)
    dma = pltpu.SemaphoreType.DMA
    bf16 = jnp.bfloat16
    vmem = pl.BlockSpec(memory_space=pltpu.VMEM)
    return pl.pallas_call(
        functools.partial(fused, groups, ctx_count, heads, reach),
        out_shape=jax.ShapeDtypeStruct((tok, out_weight.shape[1]), bf16),
        in_specs=[vmem, vmem, vmem, vmem, pl.BlockSpec(memory_space=pl.ANY)],
        out_specs=vmem,
        scratch_shapes=[
            pltpu.VMEM((reach + 1, 2, tok, keys.shape[1]), bf16),
            pltpu.VMEM((ctx_count * out_weight.shape[0], part), bf16),
            pltpu.VMEM((parts, heads * kv_heads, tok, chunk), bf16),
            pltpu.VMEM((parts - 1, tok, part), bf16),
            pltpu.VMEM((parts, tok, part), bf16),
            dma,
            dma((steps,)), dma((steps,)), dma((steps,)), dma((steps,)),
            dma, dma,
            dma((2, lines - 1, 2)), dma((2, lines - 1, 2)),
            dma((parts - 1, kv_heads)), dma((parts - 1, kv_heads)),
            dma((parts, kv_heads, heads - 1)), dma((parts, kv_heads, heads - 1)),
            dma((parts - 1,)), dma((parts - 1,)),
        ],
        compiler_params=pltpu.CompilerParams(
            collective_id=0, has_side_effects=True, vmem_limit_bytes=48 * 1024 * 1024
        ),
    )(queries, keys, values, bias, out_weight)


def solution(mesh):
    return jax.shard_map(
        per_device,
        mesh=mesh,
        in_specs=(
            P(("group", "ctx"), "head"),
            P(("group", "ctx"), "head"),
            P(("group", "ctx"), "head"),
            P("group"),
            P("ctx", "head"),
        ),
        out_specs=P(("group", "ctx"), "head"),
        check_vma=False,
    )
```

```python
import functools
import math

import jax
import jax.numpy as jnp
from jax import lax
from jax.experimental import pallas as pl
from jax.experimental.pallas import tpu as pltpu
from jax.sharding import PartitionSpec as P

HEAD_SIZE = 128
BLOCK_TOKENS = 128
MESH = pl.DeviceIdType.MESH


def fused(
    groups, ctx_count, heads, reach,
    q_hbm, k_hbm, v_hbm, doc_ref, w_ref, out_ref,
    q_ref, bias_ref, partial, in_sem, kv, wbuf, abuf, cbuf, crecv, local_sem,
    line_send, line_recv, mate_send, mate_recv,
    wmate_send, wmate_recv, wline_send, wline_recv,
    plane_send, plane_recv, core_send, core_recv, c_send, c_recv,
):
    g, c, h = lax.axis_index("group"), lax.axis_index("ctx"), lax.axis_index("head")
    x, z = lax.rem(c, 2), c // 2
    lines, steps = ctx_count // 2, reach // 2
    tok = q_ref.shape[0]
    kv_heads = k_hbm.shape[1] // HEAD_SIZE
    group_width = q_ref.shape[1] // k_hbm.shape[1]
    chunk = group_width * HEAD_SIZE
    shard = w_ref.shape[0]
    part = wbuf.shape[1]
    parts = 2 * groups
    me = g * 2 + x
    mate = c + 1 - 2 * x
    offsets = [(dg, dx) for dg in range(groups) for dx in range(2) if dg or dx]

    def copy(src, dst, send, recv, device):
        return pltpu.make_async_remote_copy(
            src_ref=src, dst_ref=dst, send_sem=send, recv_sem=recv,
            device_id=device, device_id_type=MESH,
        )

    def guarded(condition, action):
        if condition is None:
            action()
        else:
            pl.when(condition)(action)

    loads = [
        pltpu.make_async_copy(k_hbm, kv.at[0, 0], in_sem.at[0]),
        pltpu.make_async_copy(v_hbm, kv.at[0, 1], in_sem.at[1]),
        pltpu.make_async_copy(q_hbm, q_ref, in_sem.at[2]),
    ]
    for load in loads:
        load.start()
    barrier = pltpu.get_barrier_semaphore()

    def greet(device):
        pl.semaphore_signal(barrier, inc=1, device_id=device, device_id_type=MESH)

    def plane_to(dg, dx):
        return (lax.rem(g + dg, groups), 2 * z + lax.rem(x + dx, 2), h)

    def plane_from(dg, dx):
        return lax.rem(g - dg + groups, groups) * 2 + lax.rem(x + dx, 2)

    for dg, dx in offsets:
        greet(plane_to(dg, dx))
    for dh in range(1, heads):
        greet((g, c, lax.rem(h + dh, heads)))
    up, down = z + 1 < lines, z >= 1
    pl.when(up)(lambda: greet((g, c + 2, h)))
    pl.when(down)(lambda: greet((g, c - 2, h)))
    pl.semaphore_wait(
        barrier, len(offsets) + heads - 1 + up.astype(jnp.int32) + down.astype(jnp.int32)
    )

    pending = []

    def start(condition, make):
        guarded(condition, lambda: make().start())
        pending.append((condition, make))

    def received(condition, make):
        guarded(condition, lambda: make().wait_recv())

    loads[0].wait()
    loads[1].wait()

    def line_copy(s):
        return lambda: copy(
            kv.at[2 * (s - 1)], kv.at[2 * s], line_send.at[s - 1], line_recv.at[s - 1], (g, c + 2, h)
        )

    def mate_copy(m, side):
        return lambda: copy(
            kv.at[2 * m + 2 * side], kv.at[2 * m + 1], mate_send.at[m], mate_recv.at[m], (g, mate, h)
        )

    start(up, line_copy(1))
    start(x == 0, mate_copy(0, 0))

    def rows_of(source):
        return pl.ds(pl.multiple_of(source * shard, shard), shard)

    def columns_of(which):
        return pl.ds(pl.multiple_of(which * part, part), part)

    own = pltpu.make_async_copy(w_ref.at[:, columns_of(me)], wbuf.at[rows_of(c)], local_sem)
    own.start()

    def wmate_copy():
        return copy(
            w_ref.at[:, columns_of(g * 2 + 1 - x)], wbuf.at[rows_of(c)],
            wmate_send, wmate_recv, (g, mate, h),
        )

    start(None, wmate_copy)

    def wline_copy(way, s, which):
        def make():
            line = z - s if way == 0 else z + s
            source = 2 * line + (x if which == 0 else 1 - x)
            rows = rows_of(source)
            to = c + 2 if way == 0 else c - 2
            return copy(
                wbuf.at[rows], wbuf.at[rows],
                wline_send.at[way, s, which], wline_recv.at[way, s, which], (g, to, h),
            )
        return make

    def wline_sends(way, s):
        if way == 0:
            return up & (z >= s)
        return down & (z + s < lines)

    def wline_arrives(way, s):
        return z >= s + 1 if way == 0 else z + s + 1 < lines

    def pump_weights(s, halves):
        for which in halves:
            for way in range(2):
                received(wline_arrives(way, s), wline_copy(way, s, which))
                if s + 1 < lines - 1:
                    start(wline_sends(way, s + 1), wline_copy(way, s + 1, which))

    own.wait()
    start(wline_sends(1, 0), wline_copy(1, 0, 0))

    row = lax.broadcasted_iota(jnp.int32, (BLOCK_TOKENS, BLOCK_TOKENS), 0)
    col = lax.broadcasted_iota(jnp.int32, (BLOCK_TOKENS, BLOCK_TOKENS), 1)
    causal = jnp.where(col <= row, 0.0, -1e30).astype(jnp.float32)
    blocks = tok // BLOCK_TOKENS
    for d in range(reach + 1):
        first = 0 if d < reach else blocks - 1
        for kb in range(first, blocks):
            key_doc = doc_ref[jnp.maximum((c - d) * blocks + kb, 0)]
            at = d * tok + (kb - first) * BLOCK_TOKENS
            for qb in range(blocks):
                same = (key_doc == doc_ref[c * blocks + qb]) & (c >= d)
                tile = jnp.zeros_like(causal) + jnp.where(same, 0.0, -1e30).astype(jnp.float32)
                if d == 0:
                    tile = jnp.full_like(causal, -1e30) if kb > qb else tile
                    tile = jnp.minimum(tile, causal) if kb == qb else tile
                bias_ref[
                    qb * BLOCK_TOKENS:(qb + 1) * BLOCK_TOKENS, at:at + BLOCK_TOKENS
                ] = tile

    for s in range(1, steps + 1):
        received(z >= s, line_copy(s))
        if s < steps:
            start(up & (z >= s), line_copy(s + 1))
            start((x == 0) & (z >= s), mate_copy(s, 0))
        start((x == 1) & (z >= s), mate_copy(s - 1, 1))
        if s == 1:
            start(wline_sends(0, 0), wline_copy(0, 0, 0))
    received(None, wmate_copy)
    for way in (1, 0):
        start(wline_sends(way, 0), wline_copy(way, 0, 1))
    for m in range(steps):
        received(c >= 2 * m + 1, mate_copy(m, 0))
    for d in range(1, reach + 1):

        @pl.when(c < d)
        def _():
            kv[d] = jnp.zeros(kv.shape[1:], kv.dtype)

    scale = math.log2(math.e) / math.sqrt(HEAD_SIZE)

    def slot(d, which, column):
        rows = pl.ds(0, tok) if d < reach else pl.ds(tok - BLOCK_TOKENS, BLOCK_TOKENS)
        return kv[d, which, rows, column]

    def plane_copy(hk, i):
        def make():
            j = h * kv_heads + hk
            return copy(
                abuf.at[me, j], abuf.at[me, j],
                plane_send.at[i, hk], plane_recv.at[i, hk], plane_to(*offsets[i]),
            )
        return make

    def core_copy(hk, i, dh):
        def make():
            p = me if i == len(offsets) else plane_from(*offsets[i])
            j = h * kv_heads + hk
            return copy(
                abuf.at[p, j], abuf.at[p, j],
                core_send.at[i, hk, dh - 1], core_recv.at[i, hk, dh - 1],
                (g, c, lax.rem(h + dh, heads)),
            )
        return make

    def relay(hk):
        for i in range(len(offsets)):
            received(None, plane_copy(hk, i))
            for dh in range(1, heads):
                start(None, core_copy(hk, i, dh))

    loads[2].wait()
    last = lines - 2
    for s in range(last - 1):
        pump_weights(s, (0, 1))
    for hk in range(kv_heads):
        column = pl.ds(hk * HEAD_SIZE, HEAD_SIZE)

        @pl.loop(0, group_width)
        def _(n):
            at = pl.multiple_of(hk * chunk + n * HEAD_SIZE, HEAD_SIZE)
            query = q_ref[:, pl.ds(at, HEAD_SIZE)]
            scores, top = [], None
            for d in range(reach + 1):
                keys = slot(d, 0, column)
                s = lax.dot_general(
                    query, keys, (((1,), (1,)), ((), ())), preferred_element_type=jnp.float32
                )
                s = s + bias_ref[:, pl.ds(d * tok, keys.shape[0])]
                scores.append(s)
                high = jnp.max(s, axis=-1, keepdims=True)
                top = high if top is None else jnp.maximum(top, high)
            total, summed = None, None
            for d in range(reach + 1):
                weights = jnp.exp2((scores[d] - top) * scale)
                t = jnp.sum(weights, axis=-1, keepdims=True)
                o = jnp.dot(
                    weights.astype(jnp.bfloat16), slot(d, 1, column),
                    preferred_element_type=jnp.float32,
                )
                total = t if total is None else total + t
                summed = o if summed is None else summed + o
            to = pl.multiple_of(n * HEAD_SIZE, HEAD_SIZE)
            abuf[me, h * kv_heads + hk, :, pl.ds(to, HEAD_SIZE)] = (summed / total).astype(
                jnp.bfloat16
            )

        for i in reversed(range(len(offsets))):
            start(None, plane_copy(hk, i))
        for dh in range(1, heads):
            start(None, core_copy(hk, len(offsets), dh))
        if hk == kv_heads - 2 and last >= 1:
            pump_weights(last - 1, (0,))
        if hk == kv_heads - 1 and last >= 1:
            pump_weights(last - 1, (1,) if kv_heads > 1 else (0, 1))
        if hk >= 2:
            relay(hk - 2)
    for hk in range(max(kv_heads - 2, 0), kv_heads):
        relay(hk)
    for hk in range(kv_heads):
        for i in range(len(offsets) + 1):
            for dh in range(1, heads):
                received(None, core_copy(hk, i, dh))

    def c_copy(i):
        def make():
            dg, dx = offsets[i]
            return copy(cbuf.at[i], crecv.at[me], c_send.at[i], c_recv.at[i], plane_to(dg, dx))
        return make

    flip = z >= lines // 2
    far = jnp.where(flip, 0, lines - 1)

    def product(p, source):
        at = source * shard
        left = abuf[p, at // chunk, :, pl.ds(pl.multiple_of(lax.rem(at, chunk), shard), shard)]
        return jnp.dot(left, wbuf[rows_of(source), :], preferred_element_type=jnp.float32)

    for p in range(parts):
        total = None
        for source in range(2 * (lines - 1)):
            term = product(p, source + 2 * flip.astype(jnp.int32))
            total = term if total is None else total + term
        partial[p] = total
    pump_weights(last, (0, 1))

    def project(p):
        return (partial[p] + product(p, 2 * far) + product(p, 2 * far + 1)).astype(jnp.bfloat16)

    for i in reversed(range(len(offsets))):
        dg, dx = offsets[i]
        cbuf[i] = project(lax.rem(g + dg, groups) * 2 + lax.rem(x + dx, 2))
        start(None, c_copy(i))
    out_ref[:, columns_of(me)] = project(me)
    for i in reversed(range(len(offsets))):
        received(None, c_copy(i))
        source = plane_from(*offsets[i])
        out_ref[:, columns_of(source)] = crecv[source]
    for condition, make in pending:
        guarded(condition, lambda make=make: make().wait_send())


def per_device(queries, keys, values, doc_of_block, out_weight):
    tok = queries.shape[0]
    kv_heads = keys.shape[1] // HEAD_SIZE
    groups, ctx_count, heads = (lax.axis_size(a) for a in ("group", "ctx", "head"))
    reach = min(8, ctx_count // 2)
    lines, steps = ctx_count // 2, reach // 2
    parts = 2 * groups
    part = out_weight.shape[1] // parts
    chunk = queries.shape[1] // kv_heads
    window = reach * tok + BLOCK_TOKENS
    dma = pltpu.SemaphoreType.DMA
    bf16 = jnp.bfloat16
    vmem = pl.BlockSpec(memory_space=pltpu.VMEM)
    hbm = pl.BlockSpec(memory_space=pl.ANY)
    return pl.pallas_call(
        functools.partial(fused, groups, ctx_count, heads, reach),
        out_shape=jax.ShapeDtypeStruct((tok, out_weight.shape[1]), bf16),
        in_specs=[hbm, hbm, hbm, pl.BlockSpec(memory_space=pltpu.SMEM), hbm],
        out_specs=vmem,
        scratch_shapes=[
            pltpu.VMEM(queries.shape, bf16),
            pltpu.VMEM((tok, window), jnp.float32),
            pltpu.VMEM((parts, tok, part), jnp.float32),
            dma((3,)),
            pltpu.VMEM((reach + 1, 2, tok, keys.shape[1]), bf16),
            pltpu.VMEM((ctx_count * out_weight.shape[0], part), bf16),
            pltpu.VMEM((parts, heads * kv_heads, tok, chunk), bf16),
            pltpu.VMEM((parts - 1, tok, part), bf16),
            pltpu.VMEM((parts, tok, part), bf16),
            dma,
            dma((steps,)), dma((steps,)), dma((steps,)), dma((steps,)),
            dma, dma,
            dma((2, lines - 1, 2)), dma((2, lines - 1, 2)),
            dma((parts - 1, kv_heads)), dma((parts - 1, kv_heads)),
            dma((parts, kv_heads, heads - 1)), dma((parts, kv_heads, heads - 1)),
            dma((parts - 1,)), dma((parts - 1,)),
        ],
        compiler_params=pltpu.CompilerParams(
            collective_id=0, has_side_effects=True, vmem_limit_bytes=48 * 1024 * 1024
        ),
    )(queries, keys, values, doc_of_block, out_weight)


def solution(mesh):
    return jax.shard_map(
        per_device,
        mesh=mesh,
        in_specs=(
            P(("group", "ctx"), "head"),
            P(("group", "ctx"), "head"),
            P(("group", "ctx"), "head"),
            P("group"),
            P("ctx", "head"),
        ),
        out_specs=P(("group", "ctx"), "head"),
        check_vma=False,
    )
```

```python
import functools
import math

import jax
import jax.numpy as jnp
from jax import lax
from jax.experimental import pallas as pl
from jax.experimental.pallas import tpu as pltpu
from jax.sharding import PartitionSpec as P

HEAD_SIZE = 128
BLOCK_TOKENS = 128
MESH = pl.DeviceIdType.MESH


def fused(
    groups, ctx_count, heads, reach,
    q_hbm, k_hbm, v_hbm, doc_ref, w_ref, out_ref,
    q_ref, bias_ref, partial, in_sem, kv, wbuf, abuf, cbuf, crecv, local_sem,
    line_send, line_recv, mate_send, mate_recv,
    wmate_send, wmate_recv, wline_send, wline_recv,
    plane_send, plane_recv, core_send, core_recv, c_send, c_recv,
):
    g, c, h = lax.axis_index("group"), lax.axis_index("ctx"), lax.axis_index("head")
    x, z = lax.rem(c, 2), c // 2
    lines, steps = ctx_count // 2, reach // 2
    tok = q_ref.shape[0]
    kv_heads = k_hbm.shape[1] // HEAD_SIZE
    group_width = q_ref.shape[1] // k_hbm.shape[1]
    chunk = group_width * HEAD_SIZE
    shard = w_ref.shape[0]
    part = wbuf.shape[1]
    parts = 2 * groups
    me = g * 2 + x
    mate = c + 1 - 2 * x
    offsets = [(dg, dx) for dg in range(groups) for dx in range(2) if dg or dx]

    def copy(src, dst, send, recv, device):
        return pltpu.make_async_remote_copy(
            src_ref=src, dst_ref=dst, send_sem=send, recv_sem=recv,
            device_id=device, device_id_type=MESH,
        )

    def guarded(condition, action):
        if condition is None:
            action()
        else:
            pl.when(condition)(action)

    loads = [
        pltpu.make_async_copy(k_hbm, kv.at[0, 0], in_sem.at[0]),
        pltpu.make_async_copy(v_hbm, kv.at[0, 1], in_sem.at[1]),
        pltpu.make_async_copy(q_hbm, q_ref, in_sem.at[2]),
    ]
    for load in loads:
        load.start()
    barrier = pltpu.get_barrier_semaphore()

    def greet(device):
        pl.semaphore_signal(barrier, inc=1, device_id=device, device_id_type=MESH)

    def plane_to(dg, dx):
        return (lax.rem(g + dg, groups), 2 * z + lax.rem(x + dx, 2), h)

    def plane_from(dg, dx):
        return lax.rem(g - dg + groups, groups) * 2 + lax.rem(x + dx, 2)

    for dg, dx in offsets:
        greet(plane_to(dg, dx))
    for dh in range(1, heads):
        greet((g, c, lax.rem(h + dh, heads)))
    up, down = z + 1 < lines, z >= 1
    pl.when(up)(lambda: greet((g, c + 2, h)))
    pl.when(down)(lambda: greet((g, c - 2, h)))
    pl.semaphore_wait(
        barrier, len(offsets) + heads - 1 + up.astype(jnp.int32) + down.astype(jnp.int32)
    )

    pending = []

    def start(condition, make):
        guarded(condition, lambda: make().start())
        pending.append((condition, make))

    def received(condition, make):
        guarded(condition, lambda: make().wait_recv())

    loads[0].wait()
    loads[1].wait()

    def line_copy(s):
        return lambda: copy(
            kv.at[2 * (s - 1)], kv.at[2 * s], line_send.at[s - 1], line_recv.at[s - 1], (g, c + 2, h)
        )

    def mate_copy(m, side):
        return lambda: copy(
            kv.at[2 * m + 2 * side], kv.at[2 * m + 1], mate_send.at[m], mate_recv.at[m], (g, mate, h)
        )

    start(up, line_copy(1))
    start(x == 0, mate_copy(0, 0))

    def rows_of(source):
        return pl.ds(pl.multiple_of(source * shard, shard), shard)

    def columns_of(which):
        return pl.ds(pl.multiple_of(which * part, part), part)

    own = pltpu.make_async_copy(w_ref.at[:, columns_of(me)], wbuf.at[rows_of(c)], local_sem)
    own.start()

    def wmate_copy():
        return copy(
            w_ref.at[:, columns_of(g * 2 + 1 - x)], wbuf.at[rows_of(c)],
            wmate_send, wmate_recv, (g, mate, h),
        )

    start(None, wmate_copy)

    def wline_copy(way, s, which):
        def make():
            line = z - s if way == 0 else z + s
            source = 2 * line + (x if which == 0 else 1 - x)
            rows = rows_of(source)
            to = c + 2 if way == 0 else c - 2
            return copy(
                wbuf.at[rows], wbuf.at[rows],
                wline_send.at[way, s, which], wline_recv.at[way, s, which], (g, to, h),
            )
        return make

    def wline_sends(way, s):
        if way == 0:
            return up & (z >= s)
        return down & (z + s < lines)

    def wline_arrives(way, s):
        return z >= s + 1 if way == 0 else z + s + 1 < lines

    def pump_weights(s, halves, ways=(1, 0)):
        for which in halves:
            for way in ways:
                received(wline_arrives(way, s), wline_copy(way, s, which))
                if s + 1 < lines - 1:
                    start(wline_sends(way, s + 1), wline_copy(way, s + 1, which))

    last = lines - 2
    own.wait()
    for way in (1, 0):
        start(wline_sends(way, 0), wline_copy(way, 0, 0))

    row = lax.broadcasted_iota(jnp.int32, (BLOCK_TOKENS, BLOCK_TOKENS), 0)
    col = lax.broadcasted_iota(jnp.int32, (BLOCK_TOKENS, BLOCK_TOKENS), 1)
    causal = jnp.where(col <= row, 0.0, -1e30).astype(jnp.float32)
    blocks = tok // BLOCK_TOKENS
    for d in range(reach + 1):
        first = 0 if d < reach else blocks - 1
        for kb in range(first, blocks):
            key_doc = doc_ref[jnp.maximum((c - d) * blocks + kb, 0)]
            at = d * tok + (kb - first) * BLOCK_TOKENS
            for qb in range(blocks):
                same = (key_doc == doc_ref[c * blocks + qb]) & (c >= d)
                tile = jnp.zeros_like(causal) + jnp.where(same, 0.0, -1e30).astype(jnp.float32)
                if d == 0:
                    tile = jnp.full_like(causal, -1e30) if kb > qb else tile
                    tile = jnp.minimum(tile, causal) if kb == qb else tile
                bias_ref[
                    qb * BLOCK_TOKENS:(qb + 1) * BLOCK_TOKENS, at:at + BLOCK_TOKENS
                ] = tile

    for s in range(1, steps + 1):
        received(z >= s, line_copy(s))
        if s < steps:
            start(up & (z >= s), line_copy(s + 1))
            start((x == 0) & (z >= s), mate_copy(s, 0))
        start((x == 1) & (z >= s), mate_copy(s - 1, 1))
        if s == 1:
            received(None, wmate_copy)
            for way in (1, 0):
                start(wline_sends(way, 0), wline_copy(way, 0, 1))
            if last >= 2:
                pump_weights(0, (0,), (1,))
    if last >= 2:
        pump_weights(0, (1,), (1,))
        pump_weights(0, (0, 1), (0,))
    for m in range(steps):
        received(c >= 2 * m + 1, mate_copy(m, 0))
    for d in range(1, reach + 1):

        @pl.when(c < d)
        def _():
            kv[d] = jnp.zeros(kv.shape[1:], kv.dtype)

    scale = math.log2(math.e) / math.sqrt(HEAD_SIZE)

    def slot(d, which, column):
        rows = pl.ds(0, tok) if d < reach else pl.ds(tok - BLOCK_TOKENS, BLOCK_TOKENS)
        return kv[d, which, rows, column]

    def plane_copy(hk, i):
        def make():
            j = h * kv_heads + hk
            return copy(
                abuf.at[me, j], abuf.at[me, j],
                plane_send.at[i, hk], plane_recv.at[i, hk], plane_to(*offsets[i]),
            )
        return make

    def core_copy(hk, i, dh):
        def make():
            p = me if i == len(offsets) else plane_from(*offsets[i])
            j = h * kv_heads + hk
            return copy(
                abuf.at[p, j], abuf.at[p, j],
                core_send.at[i, hk, dh - 1], core_recv.at[i, hk, dh - 1],
                (g, c, lax.rem(h + dh, heads)),
            )
        return make

    def relay(hk):
        for i in range(len(offsets)):
            received(None, plane_copy(hk, i))
            for dh in range(1, heads):
                start(None, core_copy(hk, i, dh))

    loads[2].wait()
    for s in range(1, last - 1):
        pump_weights(s, (0, 1))
    for hk in range(kv_heads):
        column = pl.ds(hk * HEAD_SIZE, HEAD_SIZE)

        @pl.loop(0, group_width)
        def _(n):
            at = pl.multiple_of(hk * chunk + n * HEAD_SIZE, HEAD_SIZE)
            query = q_ref[:, pl.ds(at, HEAD_SIZE)]
            scores, top = [], None
            for d in range(reach + 1):
                keys = slot(d, 0, column)
                s = lax.dot_general(
                    query, keys, (((1,), (1,)), ((), ())), preferred_element_type=jnp.float32
                )
                s = s + bias_ref[:, pl.ds(d * tok, keys.shape[0])]
                scores.append(s)
                high = jnp.max(s, axis=-1, keepdims=True)
                top = high if top is None else jnp.maximum(top, high)
            total, summed = None, None
            for d in range(reach + 1):
                weights = jnp.exp2((scores[d] - top) * scale)
                t = jnp.sum(weights, axis=-1, keepdims=True)
                o = jnp.dot(
                    weights.astype(jnp.bfloat16), slot(d, 1, column),
                    preferred_element_type=jnp.float32,
                )
                total = t if total is None else total + t
                summed = o if summed is None else summed + o
            to = pl.multiple_of(n * HEAD_SIZE, HEAD_SIZE)
            abuf[me, h * kv_heads + hk, :, pl.ds(to, HEAD_SIZE)] = (summed / total).astype(
                jnp.bfloat16
            )

        for i in reversed(range(len(offsets))):
            start(None, plane_copy(hk, i))
        for dh in range(1, heads):
            start(None, core_copy(hk, len(offsets), dh))
        todo = [(way, which) for way in (1, 0) for which in range(2)] if last >= 1 else []
        for way, which in todo[hk * 4 // kv_heads:(hk + 1) * 4 // kv_heads]:
            pump_weights(last - 1, (which,), (way,))
        if hk >= 2:
            relay(hk - 2)
    for hk in range(max(kv_heads - 2, 0), kv_heads):
        relay(hk)
    for hk in range(kv_heads):
        for i in range(len(offsets) + 1):
            for dh in range(1, heads):
                received(None, core_copy(hk, i, dh))

    def c_copy(i):
        def make():
            dg, dx = offsets[i]
            return copy(cbuf.at[i], crecv.at[me], c_send.at[i], c_recv.at[i], plane_to(dg, dx))
        return make

    flip = z >= lines // 2
    far = jnp.where(flip, 0, lines - 1)

    def product(p, source):
        at = source * shard
        left = abuf[p, at // chunk, :, pl.ds(pl.multiple_of(lax.rem(at, chunk), shard), shard)]
        return jnp.dot(left, wbuf[rows_of(source), :], preferred_element_type=jnp.float32)

    for p in range(parts):
        total = None
        for source in range(2 * (lines - 1)):
            term = product(p, source + 2 * flip.astype(jnp.int32))
            total = term if total is None else total + term
        partial[p] = total
    pump_weights(last, (0, 1))

    def project(p):
        return (partial[p] + product(p, 2 * far) + product(p, 2 * far + 1)).astype(jnp.bfloat16)

    for i in reversed(range(len(offsets))):
        dg, dx = offsets[i]
        cbuf[i] = project(lax.rem(g + dg, groups) * 2 + lax.rem(x + dx, 2))
        start(None, c_copy(i))
    out_ref[:, columns_of(me)] = project(me)
    for i in reversed(range(len(offsets))):
        received(None, c_copy(i))
        source = plane_from(*offsets[i])
        out_ref[:, columns_of(source)] = crecv[source]
    for condition, make in pending:
        guarded(condition, lambda make=make: make().wait_send())


def per_device(queries, keys, values, doc_of_block, out_weight):
    tok = queries.shape[0]
    kv_heads = keys.shape[1] // HEAD_SIZE
    groups, ctx_count, heads = (lax.axis_size(a) for a in ("group", "ctx", "head"))
    reach = min(8, ctx_count // 2)
    lines, steps = ctx_count // 2, reach // 2
    parts = 2 * groups
    part = out_weight.shape[1] // parts
    chunk = queries.shape[1] // kv_heads
    window = reach * tok + BLOCK_TOKENS
    dma = pltpu.SemaphoreType.DMA
    bf16 = jnp.bfloat16
    vmem = pl.BlockSpec(memory_space=pltpu.VMEM)
    hbm = pl.BlockSpec(memory_space=pl.ANY)
    return pl.pallas_call(
        functools.partial(fused, groups, ctx_count, heads, reach),
        out_shape=jax.ShapeDtypeStruct((tok, out_weight.shape[1]), bf16),
        in_specs=[hbm, hbm, hbm, pl.BlockSpec(memory_space=pltpu.SMEM), hbm],
        out_specs=vmem,
        scratch_shapes=[
            pltpu.VMEM(queries.shape, bf16),
            pltpu.VMEM((tok, window), jnp.float32),
            pltpu.VMEM((parts, tok, part), jnp.float32),
            dma((3,)),
            pltpu.VMEM((reach + 1, 2, tok, keys.shape[1]), bf16),
            pltpu.VMEM((ctx_count * out_weight.shape[0], part), bf16),
            pltpu.VMEM((parts, heads * kv_heads, tok, chunk), bf16),
            pltpu.VMEM((parts - 1, tok, part), bf16),
            pltpu.VMEM((parts, tok, part), bf16),
            dma,
            dma((steps,)), dma((steps,)), dma((steps,)), dma((steps,)),
            dma, dma,
            dma((2, lines - 1, 2)), dma((2, lines - 1, 2)),
            dma((parts - 1, kv_heads)), dma((parts - 1, kv_heads)),
            dma((parts, kv_heads, heads - 1)), dma((parts, kv_heads, heads - 1)),
            dma((parts - 1,)), dma((parts - 1,)),
        ],
        compiler_params=pltpu.CompilerParams(
            collective_id=0, has_side_effects=True, vmem_limit_bytes=48 * 1024 * 1024
        ),
    )(queries, keys, values, doc_of_block, out_weight)


def solution(mesh):
    return jax.shard_map(
        per_device,
        mesh=mesh,
        in_specs=(
            P(("group", "ctx"), "head"),
            P(("group", "ctx"), "head"),
            P(("group", "ctx"), "head"),
            P("group"),
            P("ctx", "head"),
        ),
        out_specs=P(("group", "ctx"), "head"),
        check_vma=False,
    )
```
